512 devices in a mesh: dp: 8 (over y), owner: 32 (over x, z), rep: 2 (over core).
Axes of the slice: x: 4, y: 8, z: 8, core: 2. Of those that a mesh axis runs over, the one named last changes fastest.
Arguments:
- gradients: bfloat16 [8, 384, 512, 512], P('dp', None, 'owner', 'rep'), may hold values from -110 to 110
Outputs:
- updates: bfloat16 [384, 512, 512], P('owner', 'dp', 'rep')
The draws below stay inside these ranges and needn't reach their ends.
All inputs are finite; a program needn't handle non-finite values.
Results may differ from the reference program's by a relative error of at most 0.018.
Values may be sent and summed in bfloat16 or wider, within the bound.
A program may use at most 64 MiB of HBM per device.

```python
import math
import jax
import jax.numpy as jnp
from jax import lax

BS = 512
BLOCKS = 384
N_DP = 8


def draw_gradients(key, part):
    key = jax.random.fold_in(key, 11)
    key_noise = jax.random.fold_in(key, 0)
    key_rows = jax.random.fold_in(key, 2)
    key_cols = jax.random.fold_in(key, 3)
    full_shape = (N_DP, BLOCKS, BS, BS)
    ramp = 3.0 ** (jnp.arange(BS, dtype=jnp.float32) / BS)
    base = jnp.clip(jax.random.normal(key_noise, full_shape, jnp.float32), -4.0, 4.0)
    spread = math.log(10.0)
    row_scale = jnp.exp(jax.random.uniform(key_rows, (1, BLOCKS, BS, 1), jnp.float32, 0.0, spread)) * ramp[:, None]
    col_scale = jnp.exp(jax.random.uniform(key_cols, (1, BLOCKS, 1, BS), jnp.float32, 0.0, spread)) * ramp
    return (0.02 * base * row_scale * col_scale).astype(jnp.bfloat16)


def setup_inputs(seed: int = 0) -> dict:
    key_of = jax.random.split(jax.random.key(seed), 2)
    gradients = draw_gradients(jax.random.fold_in(key_of[1], 71), 0)
    return {"gradients": gradients}


def shifted(matrix, identity):
    return ((5.0 * identity - matrix.astype(jnp.float32)) * 0.25).astype(jnp.bfloat16)

def inverse_root(side_matrix):
    factor = jnp.dot(side_matrix, side_matrix.T, preferred_element_type=jnp.float32)
    fourth = 0.4 * jnp.sqrt(jnp.sum(factor * factor) + 1e-06)
    scaled = (factor / fourth).astype(jnp.bfloat16)
    identity = jnp.eye(side_matrix.shape[0], dtype=jnp.float32)
    first_shift = shifted(scaled, identity)
    square = jnp.dot(first_shift, first_shift, preferred_element_type=jnp.float32).astype(jnp.bfloat16)
    fourth_power = jnp.dot(square, square, preferred_element_type=jnp.float32).astype(jnp.bfloat16)
    next_scaled = jnp.dot(fourth_power, scaled, preferred_element_type=jnp.float32).astype(jnp.bfloat16)
    second_shift = shifted(next_scaled, identity)
    return jnp.dot(first_shift, second_shift, preferred_element_type=jnp.float32).astype(jnp.bfloat16)

def one_block(partials):
    summed = lax.optimization_barrier(jnp.sum(partials.astype(jnp.float32), axis=0)).astype(jnp.bfloat16)
    left_root = inverse_root(summed)
    right_root = inverse_root(summed.T)
    mixed = jnp.dot(left_root, summed, preferred_element_type=jnp.float32).astype(jnp.bfloat16)
    update = jnp.dot(mixed, right_root, preferred_element_type=jnp.float32)
    grad_squares = jnp.sum(jnp.square(summed.astype(jnp.float32)))
    update_squares = jnp.sum(update * update)
    return (update * (jnp.sqrt(grad_squares) / jnp.sqrt(update_squares + 1e-06))).astype(jnp.bfloat16)

def reference(gradients):

    def handle(index):
        return one_block(lax.dynamic_index_in_dim(gradients, index, 1, keepdims=False))
    return lax.map(handle, jnp.arange(BLOCKS, dtype=jnp.int32))
```

```python
import functools

import jax
import jax.numpy as jnp
from jax import lax
from jax.experimental import pallas as pl
from jax.experimental.pallas import tpu as pltpu
from jax.sharding import PartitionSpec as P

MESH = pl.DeviceIdType.MESH
BS = 512
HALF = BS // 2
F32 = jnp.float32
BF16 = jnp.bfloat16


def dot(a, b):
    return jnp.dot(a, b, preferred_element_type=F32)


def eye_shift(matrix):
    rows = lax.broadcasted_iota(jnp.int32, matrix.shape, 0)
    cols = lax.broadcasted_iota(jnp.int32, matrix.shape, 1)
    value = matrix.astype(F32) * -0.25
    return jnp.where(rows == cols, value + 1.25, value).astype(BF16)


def kernel(
    n_data,
    n_owners,
    g_ref,
    out_ref,
    own,
    ring_main,
    ring_tail,
    sums_main,
    sums_tail,
    gathered,
    side,
    scaled_ref,
    first_ref,
    root_ref,
    left_in,
    right_in,
    right_half,
    update_ref,
    norm_out,
    norm_in,
    stage,
    load_sem,
    ring_send,
    ring_recv,
    owner_send,
    owner_recv,
    half_send,
    half_recv,
    root_send,
    root_recv,
    norm_send,
    norm_recv,
    back_send,
    back_recv,
):
    y = lax.axis_index("dp")
    me = lax.axis_index("owner")
    r = lax.axis_index("rep")
    parity = lax.rem(me, 2)
    y_parity = lax.rem(y, 2)
    other = 1 - r
    subs = 4
    lead = n_owners // 2
    part = lead // subs
    row_part = BS // n_owners
    share = BS // n_data

    load = pltpu.make_async_copy(g_ref, own, load_sem)
    load.start()

    barrier = pltpu.get_barrier_semaphore()

    @pl.loop(0, n_owners)
    def _(k):
        @pl.when(k != me)
        def _():
            pl.semaphore_signal(barrier, inc=1, device_id=(y, k, r), device_id_type=MESH)

    for step in range(1, n_data):
        pl.semaphore_signal(
            barrier, inc=1, device_id=(lax.rem(y + step, n_data), me, r), device_id_type=MESH
        )
    pl.semaphore_signal(barrier, inc=1, device_id=(y, me, other), device_id_type=MESH)
    pl.semaphore_wait(barrier, n_owners + n_data - 1)

    rings = (ring_main, ring_tail)
    sums = (sums_main, sums_tail)
    neighbours = (lax.rem(y + 1, n_data), lax.rem(y + n_data - 1, n_data))

    def block_part(ref, phase, dest, c):
        lead_part = pl.ds(c * part, part)
        if phase == 0:
            return ref.at[lead_part, :, dest]
        return ref.at[lead_part, lax.rem(dest, 2), n_data + lax.div(dest, 2)]

    def dest_of(way, step):
        ahead = 4 - step if way == 0 else 4 + step
        return lax.rem(y + ahead, n_data)

    def ring_copy(phase, way, step, c, raw):
        ring = rings[phase]
        slot = ring.at[way * 4 + step, pl.ds(c * part, part)]
        if raw:
            source = block_part(g_ref, phase, dest_of(way, step), c)
        else:
            source = ring.at[way * 4 + step - 1, pl.ds(c * part, part)]
        return pltpu.make_async_remote_copy(
            src_ref=source,
            dst_ref=slot,
            send_sem=ring_send.at[phase],
            recv_sem=ring_recv.at[phase, way * 4 + step, c],
            device_id=(neighbours[way], me, r),
            device_id_type=MESH,
        )

    def ring_wait(phase, way, step, c):
        slot = rings[phase].at[way * 4 + step, pl.ds(c * part, part)]
        pltpu.make_async_copy(slot, slot, ring_recv.at[phase, way * 4 + step, c]).wait()

    first = ((0, 1), (2, 3))

    def ring_start(phase):
        for j in range(2):
            for way in range(2):
                ring_copy(phase, way, 0, first[way][j], True).start()
        for j in range(2):
            for way in range(2):
                ring_copy(phase, way, 1, first[1 - way][j], True).start()

    def ring_step(phase, way, step, c):
        ring_wait(phase, way, step, c)
        slot = rings[phase].at[way * 4 + step, pl.ds(c * part, part)]
        slot[...] = slot[...] + block_part(own, phase, dest_of(way, step + 1), c)[...]
        ring_copy(phase, way, step + 1, c, False).start()

    def ring_steps(phase):
        for step in range(3):
            order = (0, 1) if step == 0 else (2, 3, 0, 1)
            for j in order:
                for way in range(2):
                    ring_step(phase, way, step, (first[way] + first[1 - way])[j])

    def to_owner(phase, i, k):
        source = sums[phase].at[i]
        target = gathered.at[phase, r, pl.ds(me * row_part, row_part)]

        @pl.when(k != me)
        def _():
            pltpu.make_async_remote_copy(
                src_ref=source,
                dst_ref=target,
                send_sem=owner_send.at[phase],
                recv_sem=owner_recv.at[phase],
                device_id=(y, k, r),
                device_id_type=MESH,
            ).start()

        @pl.when(k == me)
        def _():
            pltpu.make_async_copy(source, target, owner_recv.at[phase]).start()

    def finish(phase):
        for c in (0, 2, 1, 3):
            for way in range(2):
                ring_wait(phase, way, 3, c)
            lead_part = pl.ds(c * part, part)
            ring = rings[phase]
            total = (
                ring[3, lead_part].astype(F32)
                + ring[7, lead_part].astype(F32)
                + block_part(own, phase, y, c)[...].astype(F32)
            ).astype(BF16)
            count = part * (2 if phase == 0 else 1)
            sums[phase][pl.ds(c * count, count)] = total.reshape(count, row_part, HALF)

            @pl.loop(0, count)
            def _(i):
                at = c * count + i
                k = at if phase == 0 else 2 * at + y_parity
                to_owner(phase, at, k)

    def precondition(phase):
        mine = gathered.at[phase, r]
        pltpu.make_async_copy(mine, mine, owner_recv.at[phase]).wait()
        swap = pltpu.make_async_remote_copy(
            src_ref=mine,
            dst_ref=mine,
            send_sem=half_send.at[phase],
            recv_sem=half_recv.at[phase],
            device_id=(y, me, other),
            device_id_type=MESH,
        )
        swap.start()
        swap.wait()

        @pl.when(r == 0)
        def _():
            for h in range(2):
                side[:, h * HALF : (h + 1) * HALF] = gathered[phase, h]

        @pl.when(r == 1)
        def _():
            for h in range(2):
                side[h * HALF : (h + 1) * HALF, :] = gathered[phase, h].T

        s = side[...]
        grad_squares = jnp.sum(jnp.square(s.astype(F32)), keepdims=True)
        factor = lax.dot_general(s, s, (((1,), (1,)), ((), ())), preferred_element_type=F32)
        fourth = 0.4 * jnp.sqrt(jnp.sum(factor * factor, keepdims=True) + 1e-06)
        scaled = (factor * (1.0 / fourth)).astype(BF16)
        scaled_ref[...] = scaled
        first_ref[...] = eye_shift(scaled)
        square = dot(first_ref[...], first_ref[...]).astype(BF16)
        power = dot(square, square).astype(BF16)
        second = eye_shift(dot(power, scaled_ref[...]).astype(BF16))

        def send_root(source, target, i):
            return pltpu.make_async_remote_copy(
                src_ref=source,
                dst_ref=target,
                send_sem=root_send.at[phase, i],
                recv_sem=root_recv.at[phase, i],
                device_id=(y, me, other),
                device_id_type=MESH,
            )

        def left_copy(h):
            rows = pl.ds(h * HALF, HALF)
            return send_root(root_ref.at[phase, rows], left_in.at[phase, rows], h)

        right_copy = send_root(right_half.at[phase], right_in.at[phase], 0)

        @pl.when(r == 0)
        def _():
            for h in range(2):
                rows = pl.ds(h * HALF, HALF)
                root_ref[phase, rows] = dot(first_ref[rows], second).astype(BF16)
                left_copy(h).start()
            mixed = dot(root_ref[phase], side[...]).astype(BF16)
            right_copy.wait_recv()
            update_ref[...] = dot(mixed, right_in[phase])
            for h in range(2):
                left_copy(h).wait_send()

        @pl.when(r == 1)
        def _():
            right_half[phase] = dot(first_ref[...], second[:, :HALF]).astype(BF16)
            right_copy.start()
            right = dot(first_ref[...], second[:, HALF:]).astype(BF16)
            mixed = (
                dot(gathered[phase, 0], right[:HALF]) + dot(gathered[phase, 1], right[HALF:])
            ).astype(BF16)
            for h in range(2):
                rows = pl.ds(h * HALF, HALF)
                left_copy(h).wait_recv()
                update_ref[rows] = dot(left_in[phase, rows], mixed)
            right_copy.wait_send()

        update = update_ref[...]
        norm = jnp.sum(update * update, keepdims=True)
        norm_out[phase] = jnp.broadcast_to(norm, (8, 128))
        norm_copy = pltpu.make_async_remote_copy(
            src_ref=norm_out.at[phase],
            dst_ref=norm_in.at[phase],
            send_sem=norm_send.at[phase],
            recv_sem=norm_recv.at[phase],
            device_id=(y, me, other),
            device_id_type=MESH,
        )
        norm_copy.start()
        norm_copy.wait()
        total = norm + norm_in[phase][0:1, 0:1]
        scale = jnp.sqrt(grad_squares) / jnp.sqrt(total + 1e-06)
        stage[phase] = (update_ref[...] * scale).astype(BF16)
        place = y if phase == 0 else n_data + lax.div(y, 2)
        for step in range(1, n_data):
            to = lax.rem(y + step, n_data)
            pltpu.make_async_remote_copy(
                src_ref=stage.at[phase, pl.ds(to * share, share)],
                dst_ref=out_ref.at[place],
                send_sem=back_send.at[phase],
                recv_sem=back_recv.at[phase],
                device_id=(to, me, r),
                device_id_type=MESH,
            ).start()
        pltpu.make_async_copy(
            stage.at[phase, pl.ds(y * share, share)], out_ref.at[place], back_recv.at[phase]
        ).start()

    has_tail = parity == y_parity

    ring_start(0)
    load.wait()
    ring_steps(0)
    ring_start(1)
    finish(0)
    ring_steps(1)
    finish(1)
    precondition(0)

    @pl.when(has_tail)
    def _():
        precondition(1)

    for phase in range(2):
        sent = rings[phase].at[pl.ds(0, 7)]
        pltpu.make_async_copy(sent, sent, ring_send.at[phase]).wait()
    sent = sums_main.at[pl.ds(0, n_owners - 1)]
    pltpu.make_async_copy(sent, sent, owner_send.at[0]).wait()

    @pl.when(has_tail)
    def _():
        sent = sums_tail.at[pl.ds(0, lead - 1)]
        pltpu.make_async_copy(sent, sent, owner_send.at[1]).wait()
        sent = stage.at[1, pl.ds(0, BS - share)]
        pltpu.make_async_copy(sent, sent, back_send.at[1]).wait()

    @pl.when(jnp.logical_not(has_tail))
    def _():
        pltpu.make_async_copy(sums_tail, sums_tail, owner_send.at[1]).wait()

    sent = stage.at[0, pl.ds(0, BS - share)]
    pltpu.make_async_copy(sent, sent, back_send.at[0]).wait()
    main_out = out_ref.at[pl.ds(0, n_data)]
    pltpu.make_async_copy(main_out, main_out, back_recv.at[0]).wait()
    tail_out = out_ref.at[pl.ds(n_data, n_data // 2)]
    pltpu.make_async_copy(tail_out, tail_out, back_recv.at[1]).wait()


def solution(mesh):
    n_data, n_owners = mesh.shape["dp"], mesh.shape["owner"]

    def on_device(gradients):
        blocks, row_part, half = gradients.shape[1:]
        slots = blocks // n_owners
        lead = n_owners // 2
        share = BS // n_data
        grouped = gradients.reshape(lead, 2, slots, row_part, half)
        vmem = pltpu.VMEM
        dma = pltpu.SemaphoreType.DMA
        return pl.pallas_call(
            functools.partial(kernel, n_data, n_owners),
            out_shape=jax.ShapeDtypeStruct((slots, share, half), BF16),
            in_specs=[pl.BlockSpec(memory_space=pl.ANY)],
            out_specs=pl.BlockSpec(memory_space=pl.ANY),
            scratch_shapes=[
                vmem((lead, 2, slots, row_part, half), BF16),
                vmem((8, lead, 2, row_part, half), BF16),
                vmem((8, lead, row_part, half), BF16),
                vmem((n_owners, row_part, half), BF16),
                vmem((lead, row_part, half), BF16),
                vmem((2, 2, BS, half), BF16),
                vmem((BS, BS), BF16),
                vmem((BS, BS), BF16),
                vmem((BS, BS), BF16),
                vmem((2, BS, BS), BF16),
                vmem((2, BS, BS), BF16),
                vmem((2, BS, half), BF16),
                vmem((2, BS, half), BF16),
                vmem((BS, half), F32),
                vmem((2, 8, 128), F32),
                vmem((2, 8, 128), F32),
                vmem((2, BS, half), BF16),
                dma,
                dma((2,)),
                dma((2, 8, 4)),
                dma((2,)),
                dma((2,)),
                dma((2,)),
                dma((2,)),
                dma((2, 2)),
                dma((2, 2)),
                dma((2,)),
                dma((2,)),
                dma((2,)),
                dma((2,)),
            ],
            compiler_params=pltpu.CompilerParams(
                collective_id=0, has_side_effects=True, vmem_limit_bytes=48 * 1024 * 1024
            ),
            name="refresh",
        )(grouped)

    return jax.shard_map(
        on_device,
        mesh=mesh,
        in_specs=(P("dp", None, "owner", "rep"),),
        out_specs=P("owner", "dp", "rep"),
        check_vma=False,
    )
```

```python
import functools

import jax
import jax.numpy as jnp
from jax import lax
from jax.experimental import pallas as pl
from jax.experimental.pallas import tpu as pltpu
from jax.sharding import PartitionSpec as P

MESH = pl.DeviceIdType.MESH
BS = 512
HALF = BS // 2
CHUNK = 128
F32 = jnp.float32
BF16 = jnp.bfloat16


def dot(a, b):
    return jnp.dot(a, b, preferred_element_type=F32)


def dot_nt(a, b):
    return lax.dot_general(a, b, (((1,), (1,)), ((), ())), preferred_element_type=F32)


def total_of(x):
    return jnp.sum(x, keepdims=True)


def kernel(
    n_data,
    n_owners,
    g_ref,
    out_ref,
    scale_ref,
    own,
    ring_main,
    ring_tail,
    sums_main,
    sums_tail,
    gathered,
    side,
    factor_ref,
    square_ref,
    cross_ref,
    power_ref,
    left_ref,
    left_in,
    right_in,
    right_half,
    right_own,
    mixed_ref,
    norm_out,
    norm_in,
    scale_out,
    stage,
    load_sem,
    ring_send,
    ring_recv,
    owner_send,
    owner_recv,
    half_send,
    half_recv,
    left_send,
    left_recv,
    right_send,
    right_recv,
    norm_send,
    norm_recv,
    back_send,
    back_recv,
    scale_send,
    scale_recv,
    round_sem,
):
    y = lax.axis_index("dp")
    me = lax.axis_index("owner")
    r = lax.axis_index("rep")
    y_parity = lax.rem(y, 2)
    has_tail = lax.rem(me, 2) == y_parity
    other = 1 - r
    subs = 4
    lead = n_owners // 2
    part = lead // subs
    row_part = BS // n_owners
    share = BS // n_data

    load = pltpu.make_async_copy(g_ref, own, load_sem)
    load.start()

    barrier = pltpu.get_barrier_semaphore()

    def owner_at(distance):
        return lax.rem(me + (distance + n_owners), n_owners)

    neighbours = (lax.rem(y + 1, n_data), lax.rem(y + n_data - 1, n_data))
    for to in neighbours:
        pl.semaphore_signal(barrier, inc=1, device_id=(to, me, r), device_id_type=MESH)
    for distance in (1, -1):
        pl.semaphore_signal(
            barrier, inc=1, device_id=(y, owner_at(distance), r), device_id_type=MESH
        )
    pl.semaphore_signal(barrier, inc=1, device_id=(y, me, other), device_id_type=MESH)
    pl.semaphore_wait(barrier, 5)

    def round_signal(i):
        for distance in (2**i, -(2**i)):
            pl.semaphore_signal(
                round_sem.at[i],
                inc=1,
                device_id=(y, owner_at(distance), r),
                device_id_type=MESH,
            )

    def round_wait(i):
        pl.semaphore_wait(round_sem.at[i], 2)

    rings = (ring_main, ring_tail)
    sums = (sums_main, sums_tail)

    def lead_of(c):
        return lax.rem(me + c, subs) * part

    def block_part(ref, phase, dest, c):
        lead_part = pl.ds(lead_of(c), part)
        if phase == 0:
            return ref.at[lead_part, :, dest]
        return ref.at[lead_part, lax.rem(dest, 2), n_data + lax.div(dest, 2)]

    def dest_of(way, step):
        ahead = 4 - step if way == 0 else 4 + step
        return lax.rem(y + ahead, n_data)

    def ring_slot(phase, way, step, c):
        return rings[phase].at[way * 4 + step, pl.ds(c * part, part)]

    def ring_copy(phase, way, step, c, raw):
        if raw:
            source = block_part(g_ref, phase, dest_of(way, step), c)
        else:
            source = ring_slot(phase, way, step - 1, c)
        return pltpu.make_async_remote_copy(
            src_ref=source,
            dst_ref=ring_slot(phase, way, step, c),
            send_sem=ring_send.at[phase],
            recv_sem=ring_recv.at[phase, way * 4 + step, c],
            device_id=(neighbours[way], me, r),
            device_id_type=MESH,
        )

    def ring_wait(phase, way, step, c):
        slot = ring_slot(phase, way, step, c)
        pltpu.make_async_copy(slot, slot, ring_recv.at[phase, way * 4 + step, c]).wait()

    long = ((0, 1), (2, 3))
    short = ((2, 3), (0, 1))

    def ring_start(phase):
        for step, parts in ((0, long), (1, short)):
            for j in range(2):
                for way in range(2):
                    ring_copy(phase, way, step, parts[way][j], True).start()

    def ring_step(phase, way, step, c):
        ring_wait(phase, way, step, c)
        slot = ring_slot(phase, way, step, c)
        slot[...] = slot[...] + block_part(own, phase, dest_of(way, step + 1), c)[...]
        ring_copy(phase, way, step + 1, c, False).start()

    def ring_steps(phase, step):
        for j in range(2 if step == 0 else 4):
            for way in range(2):
                (a, b), (c, d) = long[way], short[way]
                order = ((a, b), (c, d, a, b), (c, a, d, b))[step]
                ring_step(phase, way, step, order[j])

    def to_owner(phase, i, k):
        source = sums[phase].at[i]
        target = gathered.at[phase, r, pl.ds(me * row_part, row_part)]
        arrived = owner_recv.at[phase, lax.div(me, n_owners // 2)]

        @pl.when(k != me)
        def _():
            pltpu.make_async_remote_copy(
                src_ref=source,
                dst_ref=target,
                send_sem=owner_send.at[phase],
                recv_sem=arrived,
                device_id=(y, k, r),
                device_id_type=MESH,
            ).start()

        @pl.when(k == me)
        def _():
            pltpu.make_async_copy(source, target, arrived).start()

    def finish(phase):
        for c in (2, 0, 3, 1):
            for way in range(2):
                ring_wait(phase, way, 3, c)
            total = (
                ring_slot(phase, 0, 3, c)[...].astype(F32)
                + ring_slot(phase, 1, 3, c)[...].astype(F32)
                + block_part(own, phase, y, c)[...].astype(F32)
            ).astype(BF16)
            count = part * (2 if phase == 0 else 1)
            first = lax.rem(me + c, subs) * count
            sums[phase][pl.ds(first, count)] = total.reshape(count, row_part, HALF)

            @pl.loop(0, count)
            def _(i):
                at = first + lax.rem(i + lax.div(me, subs), count)
                k = at if phase == 0 else 2 * at + y_parity
                to_owner(phase, at, k)

    def to_core(source, target, send_sem, recv_sem):
        return pltpu.make_async_remote_copy(
            src_ref=source,
            dst_ref=target,
            send_sem=send_sem,
            recv_sem=recv_sem,
            device_id=(y, me, other),
            device_id_type=MESH,
        )

    eye = (
        lax.broadcasted_iota(jnp.int32, (CHUNK, CHUNK), 0)
        == lax.broadcasted_iota(jnp.int32, (CHUNK, CHUNK), 1)
    ).astype(F32)

    def row_chunk(j):
        chunk = lax.rem(lax.div(y, 2) + (2, 3, 1, 0)[j], BS // CHUNK)
        return chunk, pl.ds(pl.multiple_of(chunk * CHUNK, CHUNK), CHUNK)

    def precondition(phase):
        def swap(h):
            rows = gathered.at[phase, r, pl.ds(h * HALF, HALF)]
            return to_core(rows, rows, half_send.at[phase, h], half_recv.at[phase, h])

        for h in range(2):
            rows = gathered.at[phase, r, pl.ds(h * HALF, HALF)]
            pltpu.make_async_copy(rows, rows, owner_recv.at[phase, h]).wait()
            swap(h).start()
        half = gathered[phase, r]
        grad_squares = total_of(jnp.square(half.astype(F32)))

        @pl.when(r == 0)
        def _():
            side[:, :HALF] = gathered[phase, 0]

        @pl.when(r == 1)
        def _():
            side[HALF:, :] = gathered[phase, 1].T

        for h in range(2):
            swap(h).wait()

        @pl.when(r == 0)
        def _():
            side[:, HALF:] = gathered[phase, 1]

        @pl.when(r == 1)
        def _():
            side[:HALF, :] = gathered[phase, 0].T

        squares = jnp.zeros((1, 1), F32)
        for i in range(2):
            rows = pl.ds(i * HALF, HALF)
            factor = dot_nt(side[rows, :], side[...])
            squares = squares + total_of(factor * factor)
            factor_ref[rows, :] = factor.astype(BF16)
        sa = 0.5 / jnp.sqrt(squares + 1e-06)
        for i in range(2):
            rows = pl.ds(i * HALF, HALF)
            a = factor_ref[rows, :].astype(F32) * sa
            a_square = dot(factor_ref[rows, :], factor_ref[...]) * sa * sa
            cross_ref[rows, :] = (a - a_square).astype(BF16)
            square = a_square - 2.0 * a
            square_ref[rows, :] = square.astype(BF16)
            for j in range(HALF // CHUNK):
                at = i * HALF + j * CHUNK
                spot = pl.ds(at, CHUNK)
                square_ref[spot, spot] = (
                    square[j * CHUNK : (j + 1) * CHUNK, at : at + CHUNK] + eye
                ).astype(BF16)
        for i in range(2):
            rows = pl.ds(i * HALF, HALF)
            power_ref[rows, :] = dot(square_ref[rows, :], square_ref[...]).astype(BF16)

        def root_part(rows, start, cols):
            a = factor_ref[rows, cols].astype(F32) * (sa * 1.5625)
            value = dot(cross_ref[rows, :], power_ref[:, cols]) * (-(1.25**6)) - a
            row = lax.broadcasted_iota(jnp.int32, value.shape, 0) + start
            col = lax.broadcasted_iota(jnp.int32, value.shape, 1) + (cols.start or 0)
            return jnp.where(row == col, value + 1.5625, value).astype(BF16)

        def left_copy(j):
            _, rows = row_chunk(j)
            return to_core(
                left_ref.at[phase, rows],
                left_in.at[phase, rows],
                left_send.at[phase, j],
                left_recv.at[phase, j],
            )

        right_copy = to_core(
            right_half.at[phase], right_in.at[phase], right_send.at[phase], right_recv.at[phase]
        )
        place = y if phase == 0 else n_data + lax.div(y, 2)

        def send_back(j, update):
            chunk, rows = row_chunk(j)
            stage[phase, rows] = update.astype(BF16)
            for half in range(2):
                to = chunk * 2 + half
                source = stage.at[phase, pl.ds(pl.multiple_of(to * share, share), share)]

                @pl.when(to != y)
                def _():
                    pltpu.make_async_remote_copy(
                        src_ref=source,
                        dst_ref=out_ref.at[place],
                        send_sem=back_send.at[phase],
                        recv_sem=back_recv.at[phase],
                        device_id=(to, me, r),
                        device_id_type=MESH,
                    ).start()

                @pl.when(to == y)
                def _():
                    pltpu.make_async_copy(
                        source, out_ref.at[place], back_recv.at[phase]
                    ).start()

        def put_norm(norm):
            norm_out[phase, 0:4] = jnp.broadcast_to(norm, (4, 128))

        norm_out[phase, 4:8] = jnp.broadcast_to(grad_squares, (4, 128))

        @pl.when(r == 0)
        def _():
            for j in range(BS // CHUNK):
                chunk, rows = row_chunk(j)
                left_ref[phase, rows] = root_part(rows, chunk * CHUNK, slice(0, BS))
                left_copy(j).start()
            for j in range(BS // CHUNK):
                _, rows = row_chunk(j)
                mixed_ref[rows] = dot(left_ref[phase, rows], side[...]).astype(BF16)
            right_copy.wait_recv()
            norm = jnp.zeros((1, 1), F32)
            for j in range(BS // CHUNK):
                _, rows = row_chunk(j)
                update = dot(mixed_ref[rows], right_in[phase])
                send_back(j, update)
                norm = norm + total_of(update * update)
            put_norm(norm)
            for j in range(BS // CHUNK):
                left_copy(j).wait_send()

        @pl.when(r == 1)
        def _():
            for i in range(2):
                rows = pl.ds(i * HALF, HALF)
                right_half[phase, rows] = root_part(rows, i * HALF, slice(0, HALF))
            right_copy.start()
            for i in range(2):
                rows = pl.ds(i * HALF, HALF)
                right_own[rows] = root_part(rows, i * HALF, slice(HALF, BS))
            for i in range(2):
                rows = pl.ds(i * HALF, HALF)
                mixed_ref[rows, :HALF] = (
                    dot(gathered[phase, 0, rows], right_own[:HALF])
                    + dot(gathered[phase, 1, rows], right_own[HALF:])
                ).astype(BF16)
            norm = jnp.zeros((1, 1), F32)
            for j in range(BS // CHUNK):
                _, rows = row_chunk(j)
                left_copy(j).wait_recv()
                update = dot(left_in[phase, rows], mixed_ref[:, :HALF])
                send_back(j, update)
                norm = norm + total_of(update * update)
            put_norm(norm)
            right_copy.wait_send()

        norm_copy = to_core(
            norm_out.at[phase], norm_in.at[phase], norm_send.at[phase], norm_recv.at[phase]
        )
        norm_copy.start()
        norm_copy.wait()
        both = norm_out[phase] + norm_in[phase]
        scale = jnp.sqrt(both[4:5]) / jnp.sqrt(both[0:1] + 1e-06)
        scale_out[phase] = jnp.broadcast_to(scale, (8, 128))
        for distance in (4, 3, 5, 2, 6, 1, 7):
            pltpu.make_async_remote_copy(
                src_ref=scale_out.at[phase],
                dst_ref=scale_ref.at[place],
                send_sem=scale_send.at[phase],
                recv_sem=scale_recv.at[phase],
                device_id=(lax.rem(y + distance, n_data), me, r),
                device_id_type=MESH,
            ).start()
        pltpu.make_async_copy(
            scale_out.at[phase], scale_ref.at[place], scale_recv.at[phase]
        ).start()

    ring_start(0)
    round_signal(0)
    load.wait()
    ring_steps(0, 0)
    for i in range(3):
        round_wait(i)
        round_signal(i + 1)
        if i < 2:
            ring_steps(0, i + 1)
    ring_start(1)
    round_wait(3)
    finish(0)
    for step in range(3):
        ring_steps(1, step)
    finish(1)
    precondition(0)

    @pl.when(has_tail)
    def _():
        precondition(1)

    def wait_for(ref, sem):
        pltpu.make_async_copy(ref, ref, sem).wait()

    for phase in range(2):
        wait_for(rings[phase].at[pl.ds(0, 7)], ring_send.at[phase])
    wait_for(sums_main.at[pl.ds(0, n_owners - 1)], owner_send.at[0])
    wait_for(stage.at[0, pl.ds(0, BS - share)], back_send.at[0])
    wait_for(scale_ref.at[pl.ds(0, n_data - 1)], scale_send.at[0])

    @pl.when(has_tail)
    def _():
        wait_for(sums_tail.at[pl.ds(0, lead - 1)], owner_send.at[1])
        wait_for(stage.at[1, pl.ds(0, BS - share)], back_send.at[1])
        wait_for(scale_ref.at[pl.ds(0, n_data - 1)], scale_send.at[1])

    @pl.when(jnp.logical_not(has_tail))
    def _():
        wait_for(sums_tail, owner_send.at[1])

    for phase, first, count in ((0, 0, n_data), (1, n_data, n_data // 2)):
        places = pl.ds(first, count)
        wait_for(out_ref.at[places], back_recv.at[phase])
        wait_for(scale_ref.at[places], scale_recv.at[phase])


def solution(mesh):
    n_data, n_owners = mesh.shape["dp"], mesh.shape["owner"]

    def on_device(gradients):
        blocks, row_part, half = gradients.shape[1:]
        slots = blocks // n_owners
        lead = n_owners // 2
        share = BS // n_data
        grouped = gradients.reshape(lead, 2, slots, row_part, half)
        vmem = pltpu.VMEM
        dma = pltpu.SemaphoreType.DMA
        pieces, scales = pl.pallas_call(
            functools.partial(kernel, n_data, n_owners),
            out_shape=(
                jax.ShapeDtypeStruct((slots, share, half), BF16),
                jax.ShapeDtypeStruct((slots, 8, 128), F32),
            ),
            in_specs=[pl.BlockSpec(memory_space=pltpu.HBM)],
            out_specs=[pl.BlockSpec(memory_space=pl.ANY)] * 2,
            scratch_shapes=[
                vmem((lead, 2, slots, row_part, half), BF16),
                vmem((8, lead, 2, row_part, half), BF16),
                vmem((8, lead, row_part, half), BF16),
                vmem((n_owners, row_part, half), BF16),
                vmem((lead, row_part, half), BF16),
                vmem((2, 2, BS, half), BF16),
                vmem((BS, BS), BF16),
                vmem((BS, BS), BF16),
                vmem((BS, BS), BF16),
                vmem((BS, BS), BF16),
                vmem((BS, BS), BF16),
                vmem((2, BS, BS), BF16),
                vmem((2, BS, BS), BF16),
                vmem((2, BS, half), BF16),
                vmem((2, BS, half), BF16),
                vmem((BS, half), BF16),
                vmem((BS, BS), BF16),
                vmem((2, 8, 128), F32),
                vmem((2, 8, 128), F32),
                vmem((2, 8, 128), F32),
                vmem((2, BS, half), BF16),
                dma,
                dma((2,)),
                dma((2, 8, 4)),
                dma((2,)),
                dma((2, 2)),
                dma((2, 2)),
                dma((2, 2)),
                dma((2, 4)),
                dma((2, 4)),
                dma((2,)),
                dma((2,)),
                dma((2,)),
                dma((2,)),
                dma((2,)),
                dma((2,)),
                dma((2,)),
                dma((2,)),
                pltpu.SemaphoreType.REGULAR((4,)),
            ],
            compiler_params=pltpu.CompilerParams(
                collective_id=0, has_side_effects=True, vmem_limit_bytes=52 * 1024 * 1024
            ),
            name="refresh",
        )(grouped)
        return (pieces.astype(F32) * scales[:, :1, :1]).astype(BF16)

    return jax.shard_map(
        on_device,
        mesh=mesh,
        in_specs=(P("dp", None, "owner", "rep"),),
        out_specs=P("owner", "dp", "rep"),
        check_vma=False,
    )
```

```python
import functools

import jax
import jax.numpy as jnp
from jax import lax
from jax.experimental import pallas as pl
from jax.experimental.pallas import tpu as pltpu
from jax.sharding import PartitionSpec as P

MESH = pl.DeviceIdType.MESH
BS = 512
HALF = BS // 2
CHUNK = 128
F32 = jnp.float32
BF16 = jnp.bfloat16


def dot(a, b):
    return jnp.dot(a, b, preferred_element_type=F32)


def dot_nt(a, b):
    return lax.dot_general(a, b, (((1,), (1,)), ((), ())), preferred_element_type=F32)


def total_of(x):
    return jnp.sum(x, keepdims=True)


def kernel(
    n_data,
    n_owners,
    g_ref,
    out_ref,
    own,
    ring_main,
    ring_tail,
    sums_main,
    sums_tail,
    gathered,
    side,
    factor_ref,
    square_ref,
    cross_ref,
    power_ref,
    left_ref,
    left_in,
    right_in,
    right_ref,
    mixed_ref,
    partial_ref,
    sums_ref,
    update_ref,
    stage,
    load_sem,
    ring_send,
    ring_recv,
    owner_send,
    owner_recv,
    half_send,
    half_recv,
    left_send,
    left_recv,
    right_send,
    right_recv,
    back_send,
    back_recv,
    round_sem,
):
    y = lax.axis_index("dp")
    me = lax.axis_index("owner")
    r = lax.axis_index("rep")
    y_parity = lax.rem(y, 2)
    has_tail = lax.rem(me, 2) == y_parity
    other = 1 - r
    subs = 4
    lead = n_owners // 2
    part = lead // subs
    row_part = BS // n_owners
    share = BS // n_data

    load = pltpu.make_async_copy(g_ref, own, load_sem)
    load.start()

    barrier = pltpu.get_barrier_semaphore()

    def owner_at(distance):
        return lax.rem(me + (distance + n_owners), n_owners)

    neighbours = (lax.rem(y + 1, n_data), lax.rem(y + n_data - 1, n_data))
    for to in neighbours:
        pl.semaphore_signal(barrier, inc=1, device_id=(to, me, r), device_id_type=MESH)
    for distance in (1, -1):
        pl.semaphore_signal(
            barrier, inc=1, device_id=(y, owner_at(distance), r), device_id_type=MESH
        )
    pl.semaphore_signal(barrier, inc=1, device_id=(y, me, other), device_id_type=MESH)
    pl.semaphore_wait(barrier, 5)

    def round_signal(i):
        for distance in (2**i, -(2**i)):
            pl.semaphore_signal(
                round_sem.at[i],
                inc=1,
                device_id=(y, owner_at(distance), r),
                device_id_type=MESH,
            )

    def round_wait(i):
        pl.semaphore_wait(round_sem.at[i], 2)

    rings = (ring_main, ring_tail)
    sums = (sums_main, sums_tail)

    planes = (1, 0, 2, 3)
    plane_size = n_owners // subs
    my_plane = lax.div(me, plane_size)
    my_z = lax.rem(me, plane_size)

    def plane_of(c):
        return lax.rem(my_plane + planes[c], subs)

    def lead_of(c):
        return plane_of(c) * part

    def block_part(ref, phase, dest, c):
        lead_part = pl.ds(lead_of(c), part)
        if phase == 0:
            return ref.at[lead_part, :, dest]
        return ref.at[lead_part, lax.rem(dest, 2), n_data + lax.div(dest, 2)]

    def dest_of(way, step):
        ahead = 4 - step if way == 0 else 4 + step
        return lax.rem(y + ahead, n_data)

    def ring_slot(phase, way, step, c):
        return rings[phase].at[way * 4 + step, pl.ds(c * part, part)]

    def ring_copy(phase, way, step, c, raw):
        if raw:
            source = block_part(g_ref, phase, dest_of(way, step), c)
        else:
            source = ring_slot(phase, way, step - 1, c)
        return pltpu.make_async_remote_copy(
            src_ref=source,
            dst_ref=ring_slot(phase, way, step, c),
            send_sem=ring_send.at[phase],
            recv_sem=ring_recv.at[phase, way * 4 + step, c],
            device_id=(neighbours[way], me, r),
            device_id_type=MESH,
        )

    def ring_wait(phase, way, step, c):
        slot = ring_slot(phase, way, step, c)
        pltpu.make_async_copy(slot, slot, ring_recv.at[phase, way * 4 + step, c]).wait()

    long = ((0, 1), (2, 3))
    short = ((2, 3), (0, 1))

    def ring_start(phase, step, j):
        parts = (long, short)[step]
        for way in range(2):
            ring_copy(phase, way, step, parts[way][j], True).start()

    def ring_step(phase, way, step, c):
        ring_wait(phase, way, step, c)
        slot = ring_slot(phase, way, step, c)
        slot[...] = slot[...] + block_part(own, phase, dest_of(way, step + 1), c)[...]
        ring_copy(phase, way, step + 1, c, False).start()

    def ring_steps(phase, step, j):
        for way in range(2):
            (a, b), (c, d) = long[way], short[way]
            order = ((a, b), (c, d, a, b), (c, a, d, b))[step]
            ring_step(phase, way, step, order[j])

    def to_owner(phase, i, k, local):
        source = sums[phase].at[i]
        target = gathered.at[phase, r, pl.ds(me * row_part, row_part)]
        arrived = owner_recv.at[phase, lax.div(me, n_owners // 2)]
        if local:
            pltpu.make_async_copy(source, target, arrived).start()
        else:
            pltpu.make_async_remote_copy(
                src_ref=source,
                dst_ref=target,
                send_sem=owner_send.at[phase],
                recv_sem=arrived,
                device_id=(y, k, r),
                device_id_type=MESH,
            ).start()

    def finish(phase, c):
        for way in range(2):
            ring_wait(phase, way, 3, c)
        total = (
            ring_slot(phase, 0, 3, c)[...].astype(F32)
            + ring_slot(phase, 1, 3, c)[...].astype(F32)
            + block_part(own, phase, y, c)[...].astype(F32)
        ).astype(BF16)
        count = part * (2 if phase == 0 else 1)
        plane = plane_of(c)
        sums[phase][pl.ds(plane * count, count)] = total.reshape(count, row_part, HALF)
        if phase == 0:
            for distance in (4, 3, 5, 2, 6, 1, 7, 0):
                k = plane * plane_size + lax.rem(my_z + distance, plane_size)
                to_owner(0, k, k, distance == 0 and planes[c] == 0)
        else:
            for distance in (4, 2, 6, 0):
                z = lax.rem(my_z + distance + jnp.where(has_tail, 0, 1), plane_size)
                i = plane * count + lax.div(z, 2)
                k = plane * plane_size + z
                if distance == 0 and planes[c] == 0:

                    @pl.when(has_tail)
                    def _():
                        to_owner(1, i, k, True)

                    @pl.when(jnp.logical_not(has_tail))
                    def _():
                        to_owner(1, i, k, False)

                else:
                    to_owner(1, i, k, False)

    def to_core(source, target, send_sem, recv_sem):
        return pltpu.make_async_remote_copy(
            src_ref=source,
            dst_ref=target,
            send_sem=send_sem,
            recv_sem=recv_sem,
            device_id=(y, me, other),
            device_id_type=MESH,
        )

    eye = (
        lax.broadcasted_iota(jnp.int32, (CHUNK, CHUNK), 0)
        == lax.broadcasted_iota(jnp.int32, (CHUNK, CHUNK), 1)
    ).astype(F32)

    def swap(phase, h):
        rows = gathered.at[phase, r, pl.ds(h * HALF, HALF)]
        return to_core(rows, rows, half_send.at[phase, h], half_recv.at[phase, h])

    def gather(phase):
        for h in range(2):
            rows = gathered.at[phase, r, pl.ds(h * HALF, HALF)]
            pltpu.make_async_copy(rows, rows, owner_recv.at[phase, h]).wait()
            swap(phase, h).start()
        @pl.when(r == 0)
        def _():
            own_half = gathered[phase, 0]
            partial_ref[...] = dot_nt(own_half, own_half)

        @pl.when(r == 1)
        def _():
            side[HALF:, :] = gathered[phase, 1].T
            partial_ref[HALF:, HALF:] = dot_nt(side[HALF:, :], side[HALF:, :])

    def precondition(phase):
        for h in range(2):
            swap(phase, h).wait()

        def keep(parts):
            squares = jnp.zeros((1, 1), F32)
            diagonal = jnp.zeros((CHUNK, CHUNK), F32)
            for row, col, value in parts:
                height, width = value.shape
                factor_ref[row : row + height, col : col + width] = value.astype(BF16)
                squares = squares + total_of(value * value)
                for at in range(max(row, col), min(row + height, col + width), CHUNK):
                    i, j = at - row, at - col
                    diagonal = diagonal + value[i : i + CHUNK, j : j + CHUNK] * eye
            sums_ref[0:8] = jnp.broadcast_to(squares, (8, 128))
            sums_ref[8:16] = jnp.broadcast_to(total_of(diagonal), (8, 128))

        @pl.when(r == 0)
        def _():
            side[:, :HALF] = gathered[phase, 0]
            side[:, HALF:] = gathered[phase, 1]
            parts = []
            for row in (0, HALF):
                rows = slice(row, row + HALF)
                parts.append(
                    (row, 0, partial_ref[rows, :] + dot_nt(side[rows, HALF:], side[:, HALF:]))
                )
            keep(parts)

        @pl.when(r == 1)
        def _():
            side[:HALF, :] = gathered[phase, 0].T
            keep(
                (
                    (0, 0, dot_nt(side[:HALF, :], side[...])),
                    (HALF, 0, dot_nt(side[HALF:, :], side[:HALF, :])),
                    (HALF, HALF, partial_ref[HALF:, HALF:]),
                )
            )

        squares = sums_ref[0:1, 0:1]
        grad_squares = sums_ref[8:9, 0:1]
        yield
        sa = 0.5 / jnp.sqrt(squares + 1e-06)
        for i in range(2):
            rows = pl.ds(i * HALF, HALF)
            a = factor_ref[rows, :].astype(F32) * sa
            a_square = dot(factor_ref[rows, :], factor_ref[...]) * sa * sa
            cross_ref[rows, :] = (a - a_square).astype(BF16)
            square = a_square - 2.0 * a
            square_ref[rows, :] = square.astype(BF16)
            for j in range(HALF // CHUNK):
                at = i * HALF + j * CHUNK
                spot = pl.ds(at, CHUNK)
                square_ref[spot, spot] = (
                    square[j * CHUNK : (j + 1) * CHUNK, at : at + CHUNK] + eye
                ).astype(BF16)
            yield
        for i in range(2):
            rows = pl.ds(i * HALF, HALF)
            power_ref[rows, :] = dot(square_ref[rows, :], square_ref[...]).astype(BF16)
        yield

        def root_part(rows, cols):
            a = factor_ref[rows, cols].astype(F32) * (sa * 1.5625)
            value = dot(cross_ref[rows, :], power_ref[:, cols]) * (-(1.25**6)) - a
            row = lax.broadcasted_iota(jnp.int32, value.shape, 0) + rows.start
            col = lax.broadcasted_iota(jnp.int32, value.shape, 1) + cols.start
            return jnp.where(row == col, value + 1.5625, value).astype(BF16)

        halves = (slice(0, HALF), slice(HALF, BS))
        chunks = [slice(i, i + CHUNK) for i in range(0, BS, CHUNK)]

        def left_copy(j):
            rows = pl.ds(j * CHUNK, CHUNK)
            return to_core(
                left_ref.at[phase, rows],
                left_in.at[phase, rows],
                left_send.at[phase, j],
                left_recv.at[phase, j],
            )

        def right_copy(h):
            return to_core(
                right_ref.at[phase, h],
                right_in.at[phase, h],
                right_send.at[phase, h],
                right_recv.at[phase, h],
            )

        def put_norm(norm):
            sums_ref[0:8] = jnp.broadcast_to(norm, (8, 128))

        @pl.when(r == 0)
        def _():
            for j, rows in enumerate(chunks):
                left_ref[phase, rows] = root_part(rows, slice(0, BS))
                left_copy(j).start()
            for rows in halves:
                mixed_ref[rows] = dot(left_ref[phase, rows], side[...]).astype(BF16)
            norm = jnp.zeros((1, 1), F32)
            for h in range(2):
                right_copy(h).wait_recv()
                for rows in halves:
                    update = dot(mixed_ref[rows], right_in[phase, h])
                    norm = norm + total_of(update * update)
                    if h == 0:
                        update_ref[rows] = update
            put_norm(norm)

        @pl.when(r == 1)
        def _():
            for h, cols in enumerate(halves):
                for rows in halves:
                    right_ref[phase, h, rows] = root_part(rows, cols)
                right_copy(h).start()
            for h, cols in enumerate(halves):
                for rows in halves:
                    mixed_ref[rows, cols] = (
                        dot(gathered[phase, 0, rows], right_ref[phase, h, halves[0]])
                        + dot(gathered[phase, 1, rows], right_ref[phase, h, halves[1]])
                    ).astype(BF16)
            norm = jnp.zeros((1, 1), F32)
            for j, rows in enumerate(chunks):
                left_copy(j).wait_recv()
                update = dot(left_in[phase, rows], mixed_ref[...])
                norm = norm + total_of(update * update)
                update_ref[rows] = update[:, HALF:]
            put_norm(norm)

        scale = jnp.sqrt(grad_squares) / jnp.sqrt(sums_ref[0:1, 0:1] + 1e-06)
        place = y if phase == 0 else n_data + lax.div(y, 2)
        yield
        for distance in (4, 3, 5, 2, 6, 1, 7, 0):
            to = lax.rem(y + distance, n_data)
            rows = pl.ds(pl.multiple_of(to * share, share), share)
            stage[phase, rows] = (update_ref[rows] * scale).astype(BF16)
            if distance:
                pltpu.make_async_remote_copy(
                    src_ref=stage.at[phase, rows],
                    dst_ref=out_ref.at[place],
                    send_sem=back_send.at[phase],
                    recv_sem=back_recv.at[phase],
                    device_id=(to, me, r),
                    device_id_type=MESH,
                ).start()
            else:
                pltpu.make_async_copy(
                    stage.at[phase, rows], out_ref.at[place], back_recv.at[phase]
                ).start()

        @pl.when(r == 0)
        def _():
            for j in range(len(chunks)):
                left_copy(j).wait_send()

        @pl.when(r == 1)
        def _():
            for h in range(2):
                right_copy(h).wait_send()

        yield

    for step in range(2):
        for j in range(2):
            ring_start(0, step, j)
    round_signal(0)
    load.wait()
    for j in range(2):
        ring_steps(0, 0, j)
    round_wait(0)
    round_signal(1)
    for j in range(4):
        ring_steps(0, 1, j)
    round_wait(1)
    round_signal(2)
    def advance(stages, count):
        for _ in range(count):
            next(stages)

    main = precondition(0)
    ring_steps(0, 2, 0)
    ring_steps(0, 2, 1)
    ring_steps(0, 2, 2)
    ring_steps(0, 2, 3)
    ring_start(1, 0, 0)
    ring_start(1, 0, 1)
    ring_start(1, 1, 0)
    ring_start(1, 1, 1)
    round_wait(2)
    round_signal(3)
    round_wait(3)
    finish(0, 2)
    finish(0, 0)
    finish(0, 3)
    finish(0, 1)
    ring_steps(1, 0, 0)
    ring_steps(1, 0, 1)
    ring_steps(1, 1, 0)
    ring_steps(1, 1, 1)
    ring_steps(1, 1, 2)
    ring_steps(1, 1, 3)
    gather(0)
    ring_steps(1, 2, 0)
    ring_steps(1, 2, 1)
    advance(main, 1)
    ring_steps(1, 2, 2)
    advance(main, 1)
    ring_steps(1, 2, 3)
    advance(main, 1)
    finish(1, 2)
    finish(1, 0)
    advance(main, 1)
    finish(1, 3)
    finish(1, 1)
    advance(main, 1)

    @pl.when(has_tail)
    def _():
        gather(1)

    advance(main, 1)

    @pl.when(has_tail)
    def _():
        advance(precondition(1), 6)

    def wait_for(ref, sem):
        pltpu.make_async_copy(ref, ref, sem).wait()

    for phase in range(2):
        wait_for(rings[phase].at[pl.ds(0, 7)], ring_send.at[phase])
    wait_for(sums_main.at[pl.ds(0, n_owners - 1)], owner_send.at[0])
    wait_for(stage.at[0, pl.ds(0, BS - share)], back_send.at[0])

    @pl.when(has_tail)
    def _():
        wait_for(sums_tail.at[pl.ds(0, lead - 1)], owner_send.at[1])
        wait_for(stage.at[1, pl.ds(0, BS - share)], back_send.at[1])

    @pl.when(jnp.logical_not(has_tail))
    def _():
        wait_for(sums_tail, owner_send.at[1])

    for phase, first, count in ((0, 0, n_data), (1, n_data, n_data // 2)):
        places = pl.ds(first, count)
        wait_for(out_ref.at[places], back_recv.at[phase])


def solution(mesh):
    n_data, n_owners = mesh.shape["dp"], mesh.shape["owner"]

    def on_device(gradients):
        blocks, row_part, half = gradients.shape[1:]
        slots = blocks // n_owners
        lead = n_owners // 2
        share = BS // n_data
        grouped = gradients.reshape(lead, 2, slots, row_part, half)
        vmem = pltpu.VMEM
        dma = pltpu.SemaphoreType.DMA
        return pl.pallas_call(
            functools.partial(kernel, n_data, n_owners),
            out_shape=jax.ShapeDtypeStruct((slots, share, half), BF16),
            in_specs=[pl.BlockSpec(memory_space=pltpu.HBM)],
            out_specs=pl.BlockSpec(memory_space=pl.ANY),
            scratch_shapes=[
                vmem((lead, 2, slots, row_part, half), BF16),
                vmem((8, lead, 2, row_part, half), BF16),
                vmem((8, lead, row_part, half), BF16),
                vmem((n_owners, row_part, half), BF16),
                vmem((lead, row_part, half), BF16),
                vmem((2, 2, BS, half), BF16),
                vmem((BS, BS), BF16),
                vmem((BS, BS), BF16),
                vmem((BS, BS), BF16),
                vmem((BS, BS), BF16),
                vmem((BS, BS), BF16),
                vmem((2, BS, BS), BF16),
                vmem((2, BS, BS), BF16),
                vmem((2, 2, BS, half), BF16),
                vmem((2, 2, BS, half), BF16),
                vmem((BS, BS), BF16),
                vmem((BS, BS), F32),
                vmem((16, 128), F32),
                vmem((BS, half), F32),
                vmem((2, BS, half), BF16),
                dma,
                dma((2,)),
                dma((2, 8, 4)),
                dma((2,)),
                dma((2, 2)),
                dma((2, 2)),
                dma((2, 2)),
                dma((2, 4)),
                dma((2, 4)),
                dma((2, 2)),
                dma((2, 2)),
                dma((2,)),
                dma((2,)),
                pltpu.SemaphoreType.REGULAR((4,)),
            ],
            compiler_params=pltpu.CompilerParams(
                collective_id=0, has_side_effects=True, vmem_limit_bytes=52 * 1024 * 1024
            ),
            name="refresh",
        )(grouped)

    return jax.shard_map(
        on_device,
        mesh=mesh,
        in_specs=(P("dp", None, "owner", "rep"),),
        out_specs=P("owner", "dp", "rep"),
        check_vma=False,
    )
```

```python
import functools

import jax
import jax.numpy as jnp
from jax import lax
from jax.experimental import pallas as pl
from jax.experimental.pallas import tpu as pltpu
from jax.sharding import PartitionSpec as P

MESH = pl.DeviceIdType.MESH
BS = 512
HALF = BS // 2
CHUNK = 128
F32 = jnp.float32
BF16 = jnp.bfloat16


def dot(a, b):
    return jnp.dot(a, b, preferred_element_type=F32)


def dot_nt(a, b):
    return lax.dot_general(a, b, (((1,), (1,)), ((), ())), preferred_element_type=F32)


def total_of(x):
    return jnp.sum(x, keepdims=True)


def kernel(
    n_data,
    n_owners,
    g_ref,
    out_ref,
    own,
    ring_main,
    ring_tail,
    sums_main,
    sums_tail,
    gathered,
    side,
    factor_ref,
    square_ref,
    cross_ref,
    power_ref,
    left_ref,
    left_in,
    right_in,
    right_ref,
    mixed_ref,
    partial_ref,
    sums_ref,
    norms_ref,
    update_ref,
    stage,
    load_sem,
    ring_send,
    ring_recv,
    owner_send,
    owner_recv,
    half_send,
    half_recv,
    left_send,
    left_recv,
    right_send,
    right_recv,
    back_send,
    back_recv,
    round_sem,
):
    y = lax.axis_index("dp")
    me = lax.axis_index("owner")
    r = lax.axis_index("rep")
    y_parity = lax.rem(y, 2)
    has_tail = lax.rem(me, 2) == y_parity
    other = 1 - r
    subs = 4
    lead = n_owners // 2
    part = lead // subs
    row_part = BS // n_owners
    share = BS // n_data

    load = pltpu.make_async_copy(g_ref, own, load_sem)
    load.start()

    barrier = pltpu.get_barrier_semaphore()

    def owner_at(distance):
        return lax.rem(me + (distance + n_owners), n_owners)

    neighbours = (lax.rem(y + 1, n_data), lax.rem(y + n_data - 1, n_data))
    for to in neighbours:
        pl.semaphore_signal(barrier, inc=1, device_id=(to, me, r), device_id_type=MESH)
    for distance in (1, -1):
        pl.semaphore_signal(
            barrier, inc=1, device_id=(y, owner_at(distance), r), device_id_type=MESH
        )
    pl.semaphore_signal(barrier, inc=1, device_id=(y, me, other), device_id_type=MESH)
    pl.semaphore_wait(barrier, 5)

    def round_signal(i):
        for distance in (2**i, -(2**i)):
            pl.semaphore_signal(
                round_sem.at[i],
                inc=1,
                device_id=(y, owner_at(distance), r),
                device_id_type=MESH,
            )

    def round_wait(i):
        pl.semaphore_wait(round_sem.at[i], 2)

    rings = (ring_main, ring_tail)
    sums = (sums_main, sums_tail)

    planes = (1, 0, 2, 3)
    plane_size = n_owners // subs
    my_plane = lax.div(me, plane_size)
    my_z = lax.rem(me, plane_size)

    def plane_of(c):
        return lax.rem(my_plane + planes[c], subs)

    def lead_of(c):
        return plane_of(c) * part

    def block_part(ref, phase, dest, c):
        lead_part = pl.ds(lead_of(c), part)
        if phase == 0:
            return ref.at[lead_part, :, dest]
        return ref.at[lead_part, lax.rem(dest, 2), n_data + lax.div(dest, 2)]

    def dest_of(way, step):
        ahead = 4 - step if way == 0 else 4 + step
        return lax.rem(y + ahead, n_data)

    def ring_slot(phase, way, step, c):
        return rings[phase].at[way * 4 + step, pl.ds(c * part, part)]

    def ring_copy(phase, way, step, c, raw):
        if raw:
            source = block_part(g_ref, phase, dest_of(way, step), c)
        else:
            source = ring_slot(phase, way, step - 1, c)
        return pltpu.make_async_remote_copy(
            src_ref=source,
            dst_ref=ring_slot(phase, way, step, c),
            send_sem=ring_send.at[phase],
            recv_sem=ring_recv.at[phase, way * 4 + step, c],
            device_id=(neighbours[way], me, r),
            device_id_type=MESH,
        )

    def ring_wait(phase, way, step, c):
        slot = ring_slot(phase, way, step, c)
        pltpu.make_async_copy(slot, slot, ring_recv.at[phase, way * 4 + step, c]).wait()

    long = ((0, 1), (2, 3))
    short = ((2, 3), (0, 1))

    def ring_start(phase, step, j):
        parts = (long, short)[step]
        for way in range(2):
            ring_copy(phase, way, step, parts[way][j], True).start()

    def ring_step(phase, way, step, c):
        ring_wait(phase, way, step, c)
        slot = ring_slot(phase, way, step, c)
        slot[...] = slot[...] + block_part(own, phase, dest_of(way, step + 1), c)[...]
        ring_copy(phase, way, step + 1, c, False).start()

    def ring_steps(phase, step, j):
        for way in range(2):
            (a, b), (c, d) = long[way], short[way]
            order = ((a, b), (c, d, a, b), (c, a, d, b))[step]
            ring_step(phase, way, step, order[j])

    def to_owner(phase, i, k, local):
        source = sums[phase].at[i]
        target = gathered.at[phase, r, pl.ds(me * row_part, row_part)]
        arrived = owner_recv.at[phase, lax.div(me, n_owners // 2)]
        if local:
            pltpu.make_async_copy(source, target, arrived).start()
        else:
            pltpu.make_async_remote_copy(
                src_ref=source,
                dst_ref=target,
                send_sem=owner_send.at[phase],
                recv_sem=arrived,
                device_id=(y, k, r),
                device_id_type=MESH,
            ).start()

    def finish(phase, c):
        for way in range(2):
            ring_wait(phase, way, 3, c)
        total = (
            ring_slot(phase, 0, 3, c)[...].astype(F32)
            + ring_slot(phase, 1, 3, c)[...].astype(F32)
            + block_part(own, phase, y, c)[...].astype(F32)
        ).astype(BF16)
        count = part * (2 if phase == 0 else 1)
        plane = plane_of(c)
        sums[phase][pl.ds(plane * count, count)] = total.reshape(count, row_part, HALF)
        if phase == 0:
            for distance in (4, 3, 5, 2, 6, 1, 7, 0):
                k = plane * plane_size + lax.rem(my_z + distance, plane_size)
                to_owner(0, k, k, distance == 0 and planes[c] == 0)
        else:
            for distance in (4, 2, 6, 0):
                z = lax.rem(my_z + distance + jnp.where(has_tail, 0, 1), plane_size)
                i = plane * count + lax.div(z, 2)
                k = plane * plane_size + z
                if distance == 0 and planes[c] == 0:

                    @pl.when(has_tail)
                    def _():
                        to_owner(1, i, k, True)

                    @pl.when(jnp.logical_not(has_tail))
                    def _():
                        to_owner(1, i, k, False)

                else:
                    to_owner(1, i, k, False)

    def to_core(source, target, send_sem, recv_sem):
        return pltpu.make_async_remote_copy(
            src_ref=source,
            dst_ref=target,
            send_sem=send_sem,
            recv_sem=recv_sem,
            device_id=(y, me, other),
            device_id_type=MESH,
        )

    eye = (
        lax.broadcasted_iota(jnp.int32, (CHUNK, CHUNK), 0)
        == lax.broadcasted_iota(jnp.int32, (CHUNK, CHUNK), 1)
    ).astype(F32)

    def swap(phase, h):
        rows = gathered.at[phase, r, pl.ds(h * HALF, HALF)]
        return to_core(rows, rows, half_send.at[phase, h], half_recv.at[phase, h])

    def gather(phase):
        for h in range(2):
            rows = gathered.at[phase, r, pl.ds(h * HALF, HALF)]
            pltpu.make_async_copy(rows, rows, owner_recv.at[phase, h]).wait()
            swap(phase, h).start()
        @pl.when(r == 0)
        def _():
            own_half = gathered[phase, 0]
            partial_ref[...] = dot_nt(own_half, own_half)

        @pl.when(r == 1)
        def _():
            side[HALF:, :] = gathered[phase, 1].T
            partial_ref[HALF:, HALF:] = dot_nt(side[HALF:, :], side[HALF:, :])

    def precondition(phase):
        for h in range(2):
            swap(phase, h).wait()

        def keep(parts):
            squares = jnp.zeros((1, 1), F32)
            diagonal = jnp.zeros((CHUNK, CHUNK), F32)
            for row, col, value in parts:
                height, width = value.shape
                factor_ref[row : row + height, col : col + width] = value.astype(BF16)
                squares = squares + total_of(value * value)
                for at in range(max(row, col), min(row + height, col + width), CHUNK):
                    i, j = at - row, at - col
                    diagonal = diagonal + value[i : i + CHUNK, j : j + CHUNK] * eye
            sums_ref[0:8] = jnp.broadcast_to(squares, (8, 128))
            sums_ref[8:16] = jnp.broadcast_to(total_of(diagonal), (8, 128))

        @pl.when(r == 0)
        def _():
            side[:, :HALF] = gathered[phase, 0]
            side[:, HALF:] = gathered[phase, 1]
            parts = []
            for row in (0, HALF):
                rows = slice(row, row + HALF)
                parts.append(
                    (row, 0, partial_ref[rows, :] + dot_nt(side[rows, HALF:], side[:, HALF:]))
                )
            keep(parts)

        @pl.when(r == 1)
        def _():
            side[:HALF, :] = gathered[phase, 0].T
            keep(
                (
                    (0, 0, dot_nt(side[:HALF, :], side[...])),
                    (HALF, 0, dot_nt(side[HALF:, :], side[:HALF, :])),
                    (HALF, HALF, partial_ref[HALF:, HALF:]),
                )
            )

        squares = sums_ref[0:1, 0:1]
        grad_squares = sums_ref[8:9, 0:1]
        yield
        sa = 0.5 / jnp.sqrt(squares + 1e-06)
        for i in range(2):
            rows = pl.ds(i * HALF, HALF)
            a = factor_ref[rows, :].astype(F32) * sa
            a_square = dot(factor_ref[rows, :], factor_ref[...]) * sa * sa
            cross_ref[rows, :] = (a - a_square).astype(BF16)
            square = a_square - 2.0 * a
            square_ref[rows, :] = square.astype(BF16)
            for j in range(HALF // CHUNK):
                at = i * HALF + j * CHUNK
                spot = pl.ds(at, CHUNK)
                square_ref[spot, spot] = (
                    square[j * CHUNK : (j + 1) * CHUNK, at : at + CHUNK] + eye
                ).astype(BF16)
            yield
        for i in range(2):
            rows = pl.ds(i * HALF, HALF)
            power_ref[rows, :] = dot(square_ref[rows, :], square_ref[...]).astype(BF16)
            yield

        def root_part(rows, cols):
            a = factor_ref[rows, cols].astype(F32) * (sa * 1.5625)
            value = dot(cross_ref[rows, :], power_ref[:, cols]) * (-(1.25**6)) - a
            row = lax.broadcasted_iota(jnp.int32, value.shape, 0) + rows.start
            col = lax.broadcasted_iota(jnp.int32, value.shape, 1) + cols.start
            return jnp.where(row == col, value + 1.5625, value).astype(BF16)

        halves = (slice(0, HALF), slice(HALF, BS))
        chunks = [slice(i, i + CHUNK) for i in range(0, BS, CHUNK)]

        def left_copy(j):
            rows = pl.ds(j * CHUNK, CHUNK)
            return to_core(
                left_ref.at[phase, rows],
                left_in.at[phase, rows],
                left_send.at[phase, j],
                left_recv.at[phase, j],
            )

        def right_copy(h):
            return to_core(
                right_ref.at[phase, h],
                right_in.at[phase, h],
                right_send.at[phase, h],
                right_recv.at[phase, h],
            )

        norms = norms_ref.at[phase]
        for h, part_rows in enumerate((chunks[:2], chunks[2:])):

            @pl.when(r == 0)
            def _():
                for j, rows in enumerate(part_rows):
                    left_ref[phase, rows] = root_part(rows, slice(0, BS))
                    left_copy(2 * h + j).start()

            @pl.when(r == 1)
            def _():
                for rows in halves:
                    right_ref[phase, h, rows] = root_part(rows, halves[h])
                right_copy(h).start()

            yield
        for h in range(2):

            @pl.when(r == 0)
            def _():
                mixed_ref[halves[h]] = dot(left_ref[phase, halves[h]], side[...]).astype(BF16)

            @pl.when(r == 1)
            def _():
                for rows in halves:
                    mixed_ref[rows, halves[h]] = (
                        dot(gathered[phase, 0, rows], right_ref[phase, h, halves[0]])
                        + dot(gathered[phase, 1, rows], right_ref[phase, h, halves[1]])
                    ).astype(BF16)

            yield
        for h, part_rows in enumerate((chunks[:2], chunks[2:])):

            @pl.when(r == 0)
            def _():
                right_copy(h).wait_recv()
                norm = jnp.zeros((1, 1), F32)
                for rows in halves:
                    update = dot(mixed_ref[rows], right_in[phase, h])
                    norm = norm + total_of(update * update)
                    if h == 0:
                        update_ref[rows] = update
                norms[h] = jnp.broadcast_to(norm, (8, 128))

            @pl.when(r == 1)
            def _():
                norm = jnp.zeros((1, 1), F32)
                for j, rows in enumerate(part_rows):
                    left_copy(2 * h + j).wait_recv()
                    update = dot(left_in[phase, rows], mixed_ref[...])
                    norm = norm + total_of(update * update)
                    update_ref[rows] = update[:, HALF:]
                norms[h] = jnp.broadcast_to(norm, (8, 128))

            yield
        norm = norms[0, 0:1, 0:1] + norms[1, 0:1, 0:1]
        scale = jnp.sqrt(grad_squares) / jnp.sqrt(norm + 1e-06)
        place = y if phase == 0 else n_data + lax.div(y, 2)
        for distance in (4, 3, 5, 2, 6, 1, 7, 0):
            to = lax.rem(y + distance, n_data)
            rows = pl.ds(pl.multiple_of(to * share, share), share)
            stage[phase, rows] = (update_ref[rows] * scale).astype(BF16)
            if distance:
                pltpu.make_async_remote_copy(
                    src_ref=stage.at[phase, rows],
                    dst_ref=out_ref.at[place],
                    send_sem=back_send.at[phase],
                    recv_sem=back_recv.at[phase],
                    device_id=(to, me, r),
                    device_id_type=MESH,
                ).start()
            else:
                pltpu.make_async_copy(
                    stage.at[phase, rows], out_ref.at[place], back_recv.at[phase]
                ).start()

        @pl.when(r == 0)
        def _():
            for j in range(len(chunks)):
                left_copy(j).wait_send()

        @pl.when(r == 1)
        def _():
            for h in range(2):
                right_copy(h).wait_send()

        yield

    for step in range(2):
        for j in range(2):
            ring_start(0, step, j)
    round_signal(0)
    load.wait()
    for j in range(2):
        ring_steps(0, 0, j)
    round_wait(0)
    round_signal(1)
    for j in range(4):
        ring_steps(0, 1, j)
    round_wait(1)
    round_signal(2)


    def advance(stages, count):
        for _ in range(count):
            next(stages)

    main = precondition(0)
    ring_steps(0, 2, 0)
    ring_steps(0, 2, 1)
    ring_steps(0, 2, 2)
    ring_steps(0, 2, 3)
    ring_start(1, 0, 0)
    ring_start(1, 0, 1)
    ring_start(1, 1, 0)
    ring_start(1, 1, 1)
    round_wait(2)
    round_signal(3)
    round_wait(3)
    finish(0, 2)
    finish(0, 0)
    finish(0, 3)
    finish(0, 1)
    ring_steps(1, 0, 0)
    ring_steps(1, 0, 1)
    ring_steps(1, 1, 0)
    ring_steps(1, 1, 1)
    ring_steps(1, 1, 2)
    ring_steps(1, 1, 3)
    gather(0)
    ring_steps(1, 2, 0)
    ring_steps(1, 2, 1)
    ring_steps(1, 2, 2)
    ring_steps(1, 2, 3)
    advance(main, 3)
    finish(1, 2)
    finish(1, 0)
    advance(main, 3)
    finish(1, 3)
    finish(1, 1)
    advance(main, 5)

    @pl.when(has_tail)
    def _():
        gather(1)

    advance(main, 1)

    @pl.when(has_tail)
    def _():
        advance(precondition(1), 12)

    def wait_for(ref, sem):
        pltpu.make_async_copy(ref, ref, sem).wait()

    for phase in range(2):
        wait_for(rings[phase].at[pl.ds(0, 7)], ring_send.at[phase])
    wait_for(sums_main.at[pl.ds(0, n_owners - 1)], owner_send.at[0])
    wait_for(stage.at[0, pl.ds(0, BS - share)], back_send.at[0])

    @pl.when(has_tail)
    def _():
        wait_for(sums_tail.at[pl.ds(0, lead - 1)], owner_send.at[1])
        wait_for(stage.at[1, pl.ds(0, BS - share)], back_send.at[1])

    @pl.when(jnp.logical_not(has_tail))
    def _():
        wait_for(sums_tail, owner_send.at[1])

    for phase, first, count in ((0, 0, n_data), (1, n_data, n_data // 2)):
        places = pl.ds(first, count)
        wait_for(out_ref.at[places], back_recv.at[phase])


def solution(mesh):
    n_data, n_owners = mesh.shape["dp"], mesh.shape["owner"]

    def on_device(gradients):
        blocks, row_part, half = gradients.shape[1:]
        slots = blocks // n_owners
        lead = n_owners // 2
        share = BS // n_data
        grouped = gradients.reshape(lead, 2, slots, row_part, half)
        vmem = pltpu.VMEM
        dma = pltpu.SemaphoreType.DMA
        return pl.pallas_call(
            functools.partial(kernel, n_data, n_owners),
            out_shape=jax.ShapeDtypeStruct((slots, share, half), BF16),
            in_specs=[pl.BlockSpec(memory_space=pltpu.HBM)],
            out_specs=pl.BlockSpec(memory_space=pl.ANY),
            scratch_shapes=[
                vmem((lead, 2, slots, row_part, half), BF16),
                vmem((8, lead, 2, row_part, half), BF16),
                vmem((8, lead, row_part, half), BF16),
                vmem((n_owners, row_part, half), BF16),
                vmem((lead, row_part, half), BF16),
                vmem((2, 2, BS, half), BF16),
                vmem((BS, BS), BF16),
                vmem((BS, BS), BF16),
                vmem((BS, BS), BF16),
                vmem((BS, BS), BF16),
                vmem((BS, BS), BF16),
                vmem((2, BS, BS), BF16),
                vmem((2, BS, BS), BF16),
                vmem((2, 2, BS, half), BF16),
                vmem((2, 2, BS, half), BF16),
                vmem((BS, BS), BF16),
                vmem((BS, BS), F32),
                vmem((16, 128), F32),
                vmem((2, 2, 8, 128), F32),
                vmem((BS, half), F32),
                vmem((2, BS, half), BF16),
                dma,
                dma((2,)),
                dma((2, 8, 4)),
                dma((2,)),
                dma((2, 2)),
                dma((2, 2)),
                dma((2, 2)),
                dma((2, 4)),
                dma((2, 4)),
                dma((2, 2)),
                dma((2, 2)),
                dma((2,)),
                dma((2,)),
                pltpu.SemaphoreType.REGULAR((4,)),
            ],
            compiler_params=pltpu.CompilerParams(
                collective_id=0, has_side_effects=True, vmem_limit_bytes=52 * 1024 * 1024
            ),
            name="refresh",
        )(grouped)

    return jax.shard_map(
        on_device,
        mesh=mesh,
        in_specs=(P("dp", None, "owner", "rep"),),
        out_specs=P("owner", "dp", "rep"),
        check_vma=False,
    )
```

```python
import functools

import jax
import jax.numpy as jnp
from jax import lax
from jax.experimental import pallas as pl
from jax.experimental.pallas import tpu as pltpu
from jax.sharding import PartitionSpec as P

MESH = pl.DeviceIdType.MESH
BS = 512
HALF = BS // 2
CHUNK = 128
F32 = jnp.float32
BF16 = jnp.bfloat16


def dot(a, b):
    return jnp.dot(a, b, preferred_element_type=F32)


def dot_nt(a, b):
    return lax.dot_general(a, b, (((1,), (1,)), ((), ())), preferred_element_type=F32)


def total_of(x):
    return jnp.sum(x, keepdims=True)


def kernel(
    n_data,
    n_owners,
    g_ref,
    out_ref,
    own,
    ring_main,
    ring_tail,
    sums_main,
    sums_tail,
    gathered,
    side,
    factor_ref,
    square_ref,
    cross_ref,
    power_ref,
    left_ref,
    left_in,
    right_in,
    right_ref,
    mixed_ref,
    partial_ref,
    sums_ref,
    norms_ref,
    update_ref,
    stage,
    load_sem,
    ring_send,
    ring_recv,
    owner_send,
    owner_recv,
    half_send,
    half_recv,
    left_send,
    left_recv,
    right_send,
    right_recv,
    back_send,
    back_recv,
    round_sem,
):
    y = lax.axis_index("dp")
    me = lax.axis_index("owner")
    r = lax.axis_index("rep")
    y_parity = lax.rem(y, 2)
    has_tail = lax.rem(me, 2) == y_parity
    other = 1 - r
    subs = 4
    lead = n_owners // 2
    part = lead // subs
    row_part = BS // n_owners
    share = BS // n_data

    load = pltpu.make_async_copy(g_ref, own, load_sem)
    load.start()

    barrier = pltpu.get_barrier_semaphore()

    def owner_at(distance):
        return lax.rem(me + (distance + n_owners), n_owners)

    neighbours = (lax.rem(y + 1, n_data), lax.rem(y + n_data - 1, n_data))
    for to in neighbours:
        pl.semaphore_signal(barrier, inc=1, device_id=(to, me, r), device_id_type=MESH)
    for distance in (1, -1):
        pl.semaphore_signal(
            barrier, inc=1, device_id=(y, owner_at(distance), r), device_id_type=MESH
        )
    pl.semaphore_signal(barrier, inc=1, device_id=(y, me, other), device_id_type=MESH)
    pl.semaphore_wait(barrier, 5)

    def round_signal(i):
        for distance in (2**i, -(2**i)):
            pl.semaphore_signal(
                round_sem.at[i],
                inc=1,
                device_id=(y, owner_at(distance), r),
                device_id_type=MESH,
            )

    def round_wait(i):
        pl.semaphore_wait(round_sem.at[i], 2)

    rings = (ring_main, ring_tail)
    sums = (sums_main, sums_tail)

    planes = (1, 0, 2, 3)
    plane_size = n_owners // subs
    my_plane = lax.div(me, plane_size)
    my_z = lax.rem(me, plane_size)

    def plane_of(c):
        return lax.rem(my_plane + planes[c], subs)

    def lead_of(c):
        return plane_of(c) * part

    def block_part(ref, phase, dest, c):
        lead_part = pl.ds(lead_of(c), part)
        if phase == 0:
            return ref.at[lead_part, :, dest]
        return ref.at[lead_part, lax.rem(dest, 2), n_data + lax.div(dest, 2)]

    def dest_of(way, step):
        ahead = 4 - step if way == 0 else 4 + step
        return lax.rem(y + ahead, n_data)

    def ring_slot(phase, way, step, c):
        return rings[phase].at[way * 4 + step, pl.ds(c * part, part)]

    def ring_copy(phase, way, step, c, raw):
        if raw:
            source = block_part(g_ref, phase, dest_of(way, step), c)
        else:
            source = ring_slot(phase, way, step - 1, c)
        return pltpu.make_async_remote_copy(
            src_ref=source,
            dst_ref=ring_slot(phase, way, step, c),
            send_sem=ring_send.at[phase],
            recv_sem=ring_recv.at[phase, way * 4 + step, c],
            device_id=(neighbours[way], me, r),
            device_id_type=MESH,
        )

    def ring_wait(phase, way, step, c):
        slot = ring_slot(phase, way, step, c)
        pltpu.make_async_copy(slot, slot, ring_recv.at[phase, way * 4 + step, c]).wait()

    long = ((0, 1), (2, 3))
    short = ((2, 3), (0, 1))

    def ring_start(phase, step, j):
        parts = (long, short)[step]
        for way in range(2):
            ring_copy(phase, way, step, parts[way][j], True).start()

    def ring_step(phase, way, step, c):
        ring_wait(phase, way, step, c)
        slot = ring_slot(phase, way, step, c)
        slot[...] = slot[...] + block_part(own, phase, dest_of(way, step + 1), c)[...]
        ring_copy(phase, way, step + 1, c, False).start()

    def ring_steps(phase, step, j):
        for way in range(2):
            (a, b), (c, d) = long[way], short[way]
            order = ((a, b), (c, d, a, b), (c, a, d, b))[step]
            ring_step(phase, way, step, order[j])

    def to_owner(phase, i, k, local):
        source = sums[phase].at[i]
        target = gathered.at[phase, r, pl.ds(me * row_part, row_part)]
        arrived = owner_recv.at[phase, lax.div(me, n_owners // 2)]
        if local:
            pltpu.make_async_copy(source, target, arrived).start()
        else:
            pltpu.make_async_remote_copy(
                src_ref=source,
                dst_ref=target,
                send_sem=owner_send.at[phase],
                recv_sem=arrived,
                device_id=(y, k, r),
                device_id_type=MESH,
            ).start()

    def finish(phase, c):
        for way in range(2):
            ring_wait(phase, way, 3, c)
        total = (
            ring_slot(phase, 0, 3, c)[...].astype(F32)
            + ring_slot(phase, 1, 3, c)[...].astype(F32)
            + block_part(own, phase, y, c)[...].astype(F32)
        ).astype(BF16)
        count = part * (2 if phase == 0 else 1)
        plane = plane_of(c)
        sums[phase][pl.ds(plane * count, count)] = total.reshape(count, row_part, HALF)
        if phase == 0:
            for distance in (4, 3, 5, 2, 6, 1, 7, 0):
                k = plane * plane_size + lax.rem(my_z + distance, plane_size)
                to_owner(0, k, k, distance == 0 and planes[c] == 0)
        else:
            for distance in (4, 2, 6, 0):
                z = lax.rem(my_z + distance + jnp.where(has_tail, 0, 1), plane_size)
                i = plane * count + lax.div(z, 2)
                k = plane * plane_size + z
                if distance == 0 and planes[c] == 0:

                    @pl.when(has_tail)
                    def _():
                        to_owner(1, i, k, True)

                    @pl.when(jnp.logical_not(has_tail))
                    def _():
                        to_owner(1, i, k, False)

                else:
                    to_owner(1, i, k, False)

    def to_core(source, target, send_sem, recv_sem):
        return pltpu.make_async_remote_copy(
            src_ref=source,
            dst_ref=target,
            send_sem=send_sem,
            recv_sem=recv_sem,
            device_id=(y, me, other),
            device_id_type=MESH,
        )

    eye = (
        lax.broadcasted_iota(jnp.int32, (CHUNK, CHUNK), 0)
        == lax.broadcasted_iota(jnp.int32, (CHUNK, CHUNK), 1)
    ).astype(F32)

    def swap(phase, h):
        rows = gathered.at[phase, r, pl.ds(h * HALF, HALF)]
        return to_core(rows, rows, half_send.at[phase, h], half_recv.at[phase, h])

    def gather(phase):
        for h in range(2):
            rows = gathered.at[phase, r, pl.ds(h * HALF, HALF)]
            pltpu.make_async_copy(rows, rows, owner_recv.at[phase, h]).wait()
            swap(phase, h).start()
        @pl.when(r == 0)
        def _():
            own_half = gathered[phase, 0]
            partial_ref[...] = dot_nt(own_half, own_half)

        @pl.when(r == 1)
        def _():
            side[HALF:, :] = gathered[phase, 1].T
            partial_ref[HALF:, HALF:] = dot_nt(side[HALF:, :], side[HALF:, :])

    def precondition(phase):
        for h in range(2):
            swap(phase, h).wait()

        def keep(parts):
            squares = jnp.zeros((1, 1), F32)
            diagonal = jnp.zeros((CHUNK, CHUNK), F32)
            for row, col, value in parts:
                height, width = value.shape
                factor_ref[row : row + height, col : col + width] = value.astype(BF16)
                squares = squares + total_of(value * value)
                for at in range(max(row, col), min(row + height, col + width), CHUNK):
                    i, j = at - row, at - col
                    diagonal = diagonal + value[i : i + CHUNK, j : j + CHUNK] * eye
            sums_ref[0:8] = jnp.broadcast_to(squares, (8, 128))
            sums_ref[8:16] = jnp.broadcast_to(total_of(diagonal), (8, 128))

        @pl.when(r == 0)
        def _():
            side[:, :HALF] = gathered[phase, 0]
            side[:, HALF:] = gathered[phase, 1]
            parts = []
            for row in (0, HALF):
                rows = slice(row, row + HALF)
                parts.append(
                    (row, 0, partial_ref[rows, :] + dot_nt(side[rows, HALF:], side[:, HALF:]))
                )
            keep(parts)

        @pl.when(r == 1)
        def _():
            side[:HALF, :] = gathered[phase, 0].T
            keep(
                (
                    (0, 0, dot_nt(side[:HALF, :], side[...])),
                    (HALF, 0, dot_nt(side[HALF:, :], side[:HALF, :])),
                    (HALF, HALF, partial_ref[HALF:, HALF:]),
                )
            )

        squares = sums_ref[0:1, 0:1]
        grad_squares = sums_ref[8:9, 0:1]
        yield
        sa = 0.5 / jnp.sqrt(squares + 1e-06)
        for i in range(2):
            rows = pl.ds(i * HALF, HALF)
            a = factor_ref[rows, :].astype(F32) * sa
            a_square = dot(factor_ref[rows, :], factor_ref[...]) * sa * sa
            cross_ref[rows, :] = (a - a_square).astype(BF16)
            square = a_square - 2.0 * a
            square_ref[rows, :] = square.astype(BF16)
            for j in range(HALF // CHUNK):
                at = i * HALF + j * CHUNK
                spot = pl.ds(at, CHUNK)
                square_ref[spot, spot] = (
                    square[j * CHUNK : (j + 1) * CHUNK, at : at + CHUNK] + eye
                ).astype(BF16)
            yield
        for i in range(2):
            rows = pl.ds(i * HALF, HALF)
            power_ref[rows, :] = dot(square_ref[rows, :], square_ref[...]).astype(BF16)
            yield

        def root_part(rows, cols):
            a = factor_ref[rows, cols].astype(F32) * (sa * 1.5625)
            value = dot(cross_ref[rows, :], power_ref[:, cols]) * (-(1.25**6)) - a
            row = lax.broadcasted_iota(jnp.int32, value.shape, 0) + rows.start
            col = lax.broadcasted_iota(jnp.int32, value.shape, 1) + cols.start
            return jnp.where(row == col, value + 1.5625, value).astype(BF16)

        halves = (slice(0, HALF), slice(HALF, BS))
        chunks = [slice(i, i + CHUNK) for i in range(0, BS, CHUNK)]

        def left_copy(j):
            rows = pl.ds(j * CHUNK, CHUNK)
            return to_core(
                left_ref.at[phase, rows],
                left_in.at[phase, rows],
                left_send.at[phase, j],
                left_recv.at[phase, j],
            )

        def right_copy(h):
            return to_core(
                right_ref.at[phase, h],
                right_in.at[phase, h],
                right_send.at[phase, h],
                right_recv.at[phase, h],
            )

        norms = norms_ref.at[phase]
        for h, part_rows in enumerate((chunks[:2], chunks[2:])):

            @pl.when(r == 0)
            def _():
                for j, rows in enumerate(part_rows):
                    left_ref[phase, rows] = root_part(rows, slice(0, BS))
                    left_copy(2 * h + j).start()

            @pl.when(r == 1)
            def _():
                for rows in halves:
                    right_ref[phase, h, rows] = root_part(rows, halves[h])
                right_copy(h).start()

            yield
        for h in range(2):

            @pl.when(r == 0)
            def _():
                mixed_ref[halves[h]] = dot(left_ref[phase, halves[h]], side[...]).astype(BF16)

            @pl.when(r == 1)
            def _():
                for rows in halves:
                    mixed_ref[rows, halves[h]] = (
                        dot(gathered[phase, 0, rows], right_ref[phase, h, halves[0]])
                        + dot(gathered[phase, 1, rows], right_ref[phase, h, halves[1]])
                    ).astype(BF16)

            yield
        for h, part_rows in enumerate((chunks[:2], chunks[2:])):

            @pl.when(r == 0)
            def _():
                right_copy(h).wait_recv()
                norm = jnp.zeros((1, 1), F32)
                for rows in halves:
                    update = dot(mixed_ref[rows], right_in[phase, h])
                    norm = norm + total_of(update * update)
                    if h == 0:
                        update_ref[rows] = update
                norms[h] = jnp.broadcast_to(norm, (8, 128))

            @pl.when(r == 1)
            def _():
                norm = jnp.zeros((1, 1), F32)
                for j, rows in enumerate(part_rows):
                    left_copy(2 * h + j).wait_recv()
                    update = dot(left_in[phase, rows], mixed_ref[...])
                    norm = norm + total_of(update * update)
                    update_ref[rows] = update[:, HALF:]
                norms[h] = jnp.broadcast_to(norm, (8, 128))

            yield
        norm = norms[0, 0:1, 0:1] + norms[1, 0:1, 0:1]
        scale = jnp.sqrt(grad_squares) / jnp.sqrt(norm + 1e-06)
        place = y if phase == 0 else n_data + lax.div(y, 2)
        stage[phase] = (update_ref[...] * scale).astype(BF16)
        for distance in (4, 3, 5, 2, 6, 1, 7, 0):
            to = lax.rem(y + distance, n_data)
            rows = pl.ds(pl.multiple_of(to * share, share), share)
            if distance:
                pltpu.make_async_remote_copy(
                    src_ref=stage.at[phase, rows],
                    dst_ref=out_ref.at[place],
                    send_sem=back_send.at[phase],
                    recv_sem=back_recv.at[phase],
                    device_id=(to, me, r),
                    device_id_type=MESH,
                ).start()
            else:
                pltpu.make_async_copy(
                    stage.at[phase, rows], out_ref.at[place], back_recv.at[phase]
                ).start()

        @pl.when(r == 0)
        def _():
            for j in range(len(chunks)):
                left_copy(j).wait_send()

        @pl.when(r == 1)
        def _():
            for h in range(2):
                right_copy(h).wait_send()

        yield

    for step in range(2):
        for j in range(2):
            ring_start(0, step, j)
    round_signal(0)
    load.wait()
    for j in range(2):
        ring_steps(0, 0, j)
    round_wait(0)
    round_signal(1)
    for j in range(4):
        ring_steps(0, 1, j)
    round_wait(1)
    round_signal(2)


    def advance(stages, count):
        for _ in range(count):
            next(stages)

    main = precondition(0)
    ring_steps(0, 2, 0)
    ring_steps(0, 2, 1)
    ring_steps(0, 2, 2)
    ring_steps(0, 2, 3)
    ring_start(1, 0, 0)
    ring_start(1, 0, 1)
    ring_start(1, 1, 0)
    ring_start(1, 1, 1)
    round_wait(2)
    round_signal(3)
    round_wait(3)
    finish(0, 2)
    finish(0, 0)
    finish(0, 3)
    finish(0, 1)
    ring_steps(1, 0, 0)
    ring_steps(1, 0, 1)
    ring_steps(1, 1, 0)
    ring_steps(1, 1, 1)
    ring_steps(1, 1, 2)
    ring_steps(1, 1, 3)
    gather(0)
    ring_steps(1, 2, 0)
    ring_steps(1, 2, 1)
    ring_steps(1, 2, 2)
    ring_steps(1, 2, 3)
    advance(main, 3)
    finish(1, 2)
    finish(1, 0)
    advance(main, 3)
    finish(1, 3)
    finish(1, 1)
    advance(main, 5)

    @pl.when(has_tail)
    def _():
        gather(1)

    advance(main, 1)

    @pl.when(has_tail)
    def _():
        advance(precondition(1), 12)

    def wait_for(ref, sem):
        pltpu.make_async_copy(ref, ref, sem).wait()

    for phase in range(2):
        wait_for(rings[phase].at[pl.ds(0, 7)], ring_send.at[phase])
    wait_for(sums_main.at[pl.ds(0, n_owners - 1)], owner_send.at[0])
    wait_for(stage.at[0, pl.ds(0, BS - share)], back_send.at[0])

    @pl.when(has_tail)
    def _():
        wait_for(sums_tail.at[pl.ds(0, lead - 1)], owner_send.at[1])
        wait_for(stage.at[1, pl.ds(0, BS - share)], back_send.at[1])

    @pl.when(jnp.logical_not(has_tail))
    def _():
        wait_for(sums_tail, owner_send.at[1])

    for phase, first, count in ((0, 0, n_data), (1, n_data, n_data // 2)):
        places = pl.ds(first, count)
        wait_for(out_ref.at[places], back_recv.at[phase])


def solution(mesh):
    n_data, n_owners = mesh.shape["dp"], mesh.shape["owner"]

    def on_device(gradients):
        blocks, row_part, half = gradients.shape[1:]
        slots = blocks // n_owners
        lead = n_owners // 2
        share = BS // n_data
        grouped = gradients.reshape(lead, 2, slots, row_part, half)
        vmem = pltpu.VMEM
        dma = pltpu.SemaphoreType.DMA
        return pl.pallas_call(
            functools.partial(kernel, n_data, n_owners),
            out_shape=jax.ShapeDtypeStruct((slots, share, half), BF16),
            in_specs=[pl.BlockSpec(memory_space=pltpu.HBM)],
            out_specs=pl.BlockSpec(memory_space=pl.ANY),
            scratch_shapes=[
                vmem((lead, 2, slots, row_part, half), BF16),
                vmem((8, lead, 2, row_part, half), BF16),
                vmem((8, lead, row_part, half), BF16),
                vmem((n_owners, row_part, half), BF16),
                vmem((lead, row_part, half), BF16),
                vmem((2, 2, BS, half), BF16),
                vmem((BS, BS), BF16),
                vmem((BS, BS), BF16),
                vmem((BS, BS), BF16),
                vmem((BS, BS), BF16),
                vmem((BS, BS), BF16),
                vmem((2, BS, BS), BF16),
                vmem((2, BS, BS), BF16),
                vmem((2, 2, BS, half), BF16),
                vmem((2, 2, BS, half), BF16),
                vmem((BS, BS), BF16),
                vmem((BS, BS), F32),
                vmem((16, 128), F32),
                vmem((2, 2, 8, 128), F32),
                vmem((BS, half), F32),
                vmem((2, BS, half), BF16),
                dma,
                dma((2,)),
                dma((2, 8, 4)),
                dma((2,)),
                dma((2, 2)),
                dma((2, 2)),
                dma((2, 2)),
                dma((2, 4)),
                dma((2, 4)),
                dma((2, 2)),
                dma((2, 2)),
                dma((2,)),
                dma((2,)),
                pltpu.SemaphoreType.REGULAR((4,)),
            ],
            compiler_params=pltpu.CompilerParams(
                collective_id=0, has_side_effects=True, vmem_limit_bytes=52 * 1024 * 1024
            ),
            name="refresh",
        )(grouped)

    return jax.shard_map(
        on_device,
        mesh=mesh,
        in_specs=(P("dp", None, "owner", "rep"),),
        out_specs=P("owner", "dp", "rep"),
        check_vma=False,
    )
```
